256 devices in a mesh: section: 16 (over z, x_lo), seq: 16 (over x_hi, y, core).
Axes of the slice: x: 4 (x_hi: 2, x_lo: 2; x = x_hi * 2 + x_lo), y: 4, z: 8, core: 2. Of those that a mesh axis runs over, the one named last changes fastest.
Arguments:
- forward_layer_inputs: bfloat16 [16, 2048, 3584], P('section', 'seq'), may hold values from -6 to 6
- backward_layer_inputs: bfloat16 [16, 2048, 3584], P('section', 'seq'), may hold values from -6 to 6
- output_cotangent: bfloat16 [16, 2048, 3584], P('section', 'seq'), may hold values from -6 to 6
- embeds: bfloat16 [2, 2048, 3584], P(None, 'seq', 'section'), may hold values from -6 to 6
- roster: int32 [16, 2], P('section'), may hold values from 0 to 1
- shared: int32 [16], P('section'), may hold values 0 or 1
- step_key_query_weight: bfloat16 [16, 3584, 184], P('section'), may hold values from -0.09375 to 0.09375
- head_step_bias: float32 [16, 56], P('section'), may hold values from -1.5 to 0.5
- rate: float32 [16, 56], P('section'), may hold values from 0.0005 to 0.1
- dskip: float32 [16, 56], P('section'), may hold values from 0.5 to 1.5
- gain: float32 [16, 3584], P('section'), may hold values from 0.5 to 1.5
- adapter_down_map: bfloat16 [16, 7168, 128], P('section'), may hold values from -0.0625 to 0.0625
- adapter_up_map: bfloat16 [16, 128, 3584], P('section'), may hold values from -0.5 to 0.5
Outputs:
- fwd_next: bfloat16 [16, 2048, 3584], P('section', 'seq')
- grad_prev: bfloat16 [16, 2048, 3584], P('section', 'seq')
- grad_w_small: bfloat16 [16, 3584, 184], P('section', 'seq')
- grad_lora_a: bfloat16 [16, 7168, 128], P('section', 'seq')
- grad_lora_b: bfloat16 [16, 128, 3584], P('section', 'seq')
The draws below stay inside these ranges and needn't reach their ends.
All inputs are finite; a program needn't handle non-finite values. No bound on the sum of `shared` on one device may be relied on, other than what follows from the above.
Results may differ from the reference program's by a relative error of at most 0.02.
Values may be sent and summed in bfloat16 or wider, within the bound.
No kernel may reach another device: no remote copies, remote signals or barrier semaphores. Data moves between devices by JAX's collectives and lax.ppermute only.
A program may use at most 192 MiB of HBM per device.

```python
import math
import jax
import jax.numpy as jnp
from jax import lax

HEADS = 56
HEAD_DIM = 64
STATE = 64
ADAPTER_RANK = 128
TOK_DEV = 128
MBS = 2
MODEL_WIDTH = 3584
PROJ = 184
WINDOW_LAYERS = 16
LEN = 2048
N_SEQ = 16


def place_ends(values, key, least, high):
    place = [jax.random.randint(jax.random.fold_in(key, axis), (), 0, length) for axis, length in enumerate(values.shape)]
    main_axis = values.shape.index(max(values.shape))
    beside = place[:main_axis] + [(place[main_axis] + 1) % values.shape[main_axis]] + place[main_axis + 1:]
    return values.at[tuple(place)].set(least).at[tuple(beside)].set(high)


def steps_of(key, dims, cuts, least, largest):
    def one(position, shards_of):
        steps = jax.random.uniform(jax.random.fold_in(jax.random.fold_in(key, 6), position), (shards_of,), jnp.float32, least / len(cuts), largest / len(cuts))
        return jnp.repeat(jnp.exp(steps), dims[position] // shards_of).reshape((-1,) + (1,) * (len(dims) - position - 1))

    level = one(*cuts[0])
    for cut in cuts[1:]:
        level = level * one(*cut)
    return level


def gaussian(stream_key, shape, scale, bound, pieces=(), dtype=jnp.bfloat16):
    values = scale * jax.random.normal(stream_key, shape, jnp.float32)
    if pieces:
        values = values * steps_of(stream_key, shape, pieces, -0.22, 0.18)
    return jnp.clip(values, -bound, bound).astype(dtype)


def setup_inputs(seed: int = 0) -> dict:
    seeds = jax.random.split(jax.random.key(seed), 14)
    forward_layer_inputs = gaussian(seeds[0], (WINDOW_LAYERS, LEN, MODEL_WIDTH), 1.0, 6.0, ((0, 16), (1, 16)))
    backward_layer_inputs = gaussian(seeds[1], (WINDOW_LAYERS, LEN, MODEL_WIDTH), 1.0, 6.0, ((0, 16), (1, 16)))
    output_cotangent = gaussian(seeds[2], (WINDOW_LAYERS, LEN, MODEL_WIDTH), 1.0, 6.0, ((0, 16), (1, 16)))
    embeds = gaussian(seeds[3], (MBS, LEN, MODEL_WIDTH), 1.0, 6.0, ((1, 16), (2, 16)))
    roster = place_ends(jax.random.randint(seeds[4], (WINDOW_LAYERS, 2), 0, MBS), jax.random.fold_in(seeds[4], 1), 0, MBS - 1).astype(jnp.int32)
    shared = place_ends((jax.random.randint(seeds[5], (WINDOW_LAYERS,), 0, 2) < 1).astype(jnp.int32), jax.random.fold_in(seeds[5], 1), 0, 1)
    step_key_query_weight = gaussian(seeds[6], (WINDOW_LAYERS, MODEL_WIDTH, PROJ), MODEL_WIDTH ** -0.5, 0.09375, ((0, 16),))
    head_step_bias = jnp.clip(-1.5 + 2.0 * jax.random.uniform(seeds[7], (WINDOW_LAYERS, HEADS), jnp.float32) ** steps_of(seeds[7], (WINDOW_LAYERS, HEADS), ((0, 16),), -0.2, 0.2), -1.5, 0.5)
    rate = jnp.clip(jnp.exp(math.log(0.1) - 5.2983173 * jax.random.uniform(seeds[8], (WINDOW_LAYERS, HEADS), jnp.float32) ** steps_of(seeds[8], (WINDOW_LAYERS, HEADS), ((0, 16),), -0.2, 0.2)), 0.0005, 0.1)
    dskip = jnp.clip(0.5 + 1.0 * jax.random.uniform(seeds[9], (WINDOW_LAYERS, HEADS), jnp.float32) ** steps_of(seeds[9], (WINDOW_LAYERS, HEADS), ((0, 16),), -0.2, 0.2), 0.5, 1.5)
    gain = jnp.clip(1.0 + 0.1 * jax.random.normal(seeds[10], (WINDOW_LAYERS, MODEL_WIDTH), jnp.float32), 0.5, 1.5)
    adapter_down_map = gaussian(seeds[11], (WINDOW_LAYERS, 2 * MODEL_WIDTH, ADAPTER_RANK), (2 * MODEL_WIDTH) ** -0.5, 0.0625, ((0, 16),))
    adapter_up_map = gaussian(seeds[12], (WINDOW_LAYERS, ADAPTER_RANK, MODEL_WIDTH), ADAPTER_RANK ** -0.5, 0.5, ((0, 16),))
    return {"forward_layer_inputs": forward_layer_inputs, "backward_layer_inputs": backward_layer_inputs, "output_cotangent": output_cotangent, "embeds": embeds, "roster": roster, "shared": shared, "step_key_query_weight": step_key_query_weight, "head_step_bias": head_step_bias, "rate": rate, "dskip": dskip, "gain": gain, "adapter_down_map": adapter_down_map, "adapter_up_map": adapter_up_map}


EPS = 1e-05
HIGH = lax.Precision.HIGHEST

def matmul(left, right):
    return jnp.dot(left, right, preferred_element_type=jnp.float32)

def features(proj, head_step_bias, rate):
    heads = head_step_bias.shape[0]
    width = (proj.shape[1] - heads) // 2
    step = jax.nn.softplus(proj[:, :heads] + head_step_bias)
    keys = proj[:, heads:heads + width]
    queries = proj[:, heads + width:]
    logd = jnp.cumsum(-rate * step, axis=0)
    return (step, keys, queries, logd)

def group_state(vecf, step, keys, logd):
    rows, heads = step.shape
    inputs = vecf.reshape(rows, heads, -1)
    weight = jnp.exp(logd[-1] - logd) * step
    state = jnp.einsum('ch,chp,cn->hpn', weight, inputs, keys, precision=HIGH)
    return (state, jnp.exp(logd[-1]))

def group_out(vecf, step, keys, queries, logd, start_state, dskip, gain):
    rows, heads = step.shape
    inputs = vecf.reshape(rows, heads, -1)
    inter = jnp.einsum('cn,hpn->chp', queries, start_state, precision=HIGH) * jnp.exp(logd)[:, :, None]
    scores = jnp.dot(queries, keys.T, precision=HIGH)
    lower = (jnp.arange(rows)[:, None] >= jnp.arange(rows)[None, :])[:, :, None]
    gap = jnp.where(lower, logd[:, None, :] - logd[None, :, :], 0.0)
    mix = jnp.where(lower, jnp.exp(gap), 0.0) * scores[:, :, None] * step[None, :, :]
    intra = jnp.einsum('sth,thp->shp', mix, inputs, precision=HIGH)
    result = (inter + intra + dskip[None, :, None] * inputs).reshape(rows, -1)
    normed = result * lax.rsqrt(lax.optimization_barrier(jnp.mean(result * result, axis=1, keepdims=True)) + EPS)
    return vecf + gain * normed

def middle(proj, vecf, head_step_bias, rate, dskip, gain):
    blocks_p = proj.reshape(N_SEQ, TOK_DEV, proj.shape[1])
    blocks_v = vecf.reshape(N_SEQ, TOK_DEV, vecf.shape[1])
    start = jnp.zeros((head_step_bias.shape[0], HEAD_DIM, STATE), jnp.float32)

    def advance(carry, pair):
        piece_p, piece_v = pair
        step, keys, queries, logd = features(piece_p, head_step_bias, rate)
        state, decay = group_state(piece_v, step, keys, logd)
        result = group_out(piece_v, step, keys, queries, logd, carry, dskip, gain)
        return (decay[:, None, None] * carry + state, result)
    _, outs = lax.scan(advance, start, (blocks_p, blocks_v))
    return outs.reshape(proj.shape[0], -1)

def reference(forward_layer_inputs, backward_layer_inputs, output_cotangent, embeds, roster, shared, step_key_query_weight, head_step_bias, rate, dskip, gain, adapter_down_map, adapter_up_map):

    def section_index(items):
        u_f, u_b, cotan, plan, flag, weight, bias, decay_rate, skip, norm_gain, down_product, up_product = items
        flagf = flag.astype(jnp.float32)

        def front(tokens, emb):
            both = jnp.concatenate([tokens, emb], axis=1)
            low = matmul(both, down_product).astype(jnp.bfloat16)
            vec = (tokens.astype(jnp.float32) + flagf * matmul(low, up_product)).astype(jnp.bfloat16)
            return (both, low, vec, matmul(vec, weight))
        _, _, vec_f, proj_f = front(u_f, embeds[plan[0]])
        out_f = middle(proj_f, vec_f.astype(jnp.float32), bias, decay_rate, skip, norm_gain).astype(jnp.bfloat16)
        both_b, low_b, vec_b, proj_b = front(u_b, embeds[plan[1]])
        _, pull = jax.vjp(lambda p, v: middle(p, v, bias, decay_rate, skip, norm_gain), proj_b, vec_b.astype(jnp.float32))
        d_proj, d_vecf = pull(cotan.astype(jnp.float32))
        d_proj = d_proj.astype(jnp.bfloat16)
        d_vec = (d_vecf + matmul(d_proj, weight.T)).astype(jnp.bfloat16)
        projection_gradient = matmul(vec_b.T, d_proj)
        up_map_gradient = flagf * matmul(low_b.T, d_vec)
        d_low = (flagf * matmul(d_vec, up_product.T)).astype(jnp.bfloat16)
        down_map_gradient = matmul(both_b.T, d_low)
        d_both = matmul(d_low, down_product.T)
        d_tokens = (d_vec.astype(jnp.float32) + d_both[:, :MODEL_WIDTH]).astype(jnp.bfloat16)
        return (out_f, d_tokens, projection_gradient.astype(jnp.bfloat16), down_map_gradient.astype(jnp.bfloat16), up_map_gradient.astype(jnp.bfloat16))
    forward_outputs, input_gradient, projection_gradient, down_map_gradient, up_map_gradient = lax.map(section_index, (forward_layer_inputs, backward_layer_inputs, output_cotangent, roster, shared, step_key_query_weight, head_step_bias, rate, dskip, gain, adapter_down_map, adapter_up_map))
    return (jnp.roll(forward_outputs, 1, axis=0), jnp.roll(input_gradient, -1, axis=0), projection_gradient, down_map_gradient, up_map_gradient)
```

```python
import jax
import jax.numpy as jnp
from jax import lax
from jax.experimental import pallas as pl
from jax.experimental.pallas import tpu as pltpu
from jax.sharding import PartitionSpec as P

EPS = 1e-05
HIGH = lax.Precision.HIGHEST
F32 = jnp.float32
BF16 = jnp.bfloat16

TOK = 128
HEADS = 56
CH = 64
WIDTH = 3584
RANK = 128
PROJ = 184
N = 16
BLOCKS = WIDTH // 128
STEP = 512
CHUNKS = WIDTH // STEP
SROWS = BLOCKS * CH // N
SHARD = WIDTH // N
GA, GWA, GWB, GB = 448, 224, 112, 224
OFF_WA = GA
OFF_WB = GA + GWA
OFF_B = OFF_WB + GWB
PACK = OFF_B + GB
MIB = 1024 * 1024
SMALL, BIG = 40, 62


def nn(a, b, precision=None):
    return lax.dot_general(
        a, b, (((1,), (0,)), ((), ())), preferred_element_type=F32, precision=precision
    )


def nt(a, b, precision=None):
    return lax.dot_general(
        a, b, (((1,), (1,)), ((), ())), preferred_element_type=F32, precision=precision
    )


def tn(a, b, precision=None):
    return lax.dot_general(
        a, b, (((0,), (0,)), ((), ())), preferred_element_type=F32, precision=precision
    )


def iota(shape, axis):
    return lax.broadcasted_iota(jnp.int32, shape, axis)


def split(a):
    hi = a.astype(BF16)
    return hi, (a - hi.astype(F32)).astype(BF16)


def head_map(chunk):
    head = iota((HEADS, STEP), 0)
    lane = iota((HEADS, STEP), 1) + chunk * STEP
    return jnp.where(head == lane // CH, 1.0, 0.0).astype(BF16)


def expand(parts, table):
    return nn(parts[0], table) + nn(parts[1], table)


def segment(a, table):
    hi, lo = split(a)
    return nt(hi, table) + nt(lo, table)


def softplus(z):
    return jnp.maximum(z, 0.0) + jnp.log1p(jnp.exp(-jnp.abs(z)))


def features(proj, bias, rate):
    z = proj[:, :HEADS] + bias
    step = softplus(z)
    keys = proj[:, HEADS : HEADS + CH]
    queries = proj[:, HEADS + CH :]
    row = iota((TOK, TOK), 0)
    col = iota((TOK, TOK), 1)
    a = -rate * step
    logd = nn(jnp.where(row >= col, 1.0, 0.0), a, HIGH)
    return z, step, keys, queries, logd


def turned(step, logd):
    row = iota((TOK, TOK), 0)
    col = iota((TOK, TOK), 1)
    eye = jnp.where(row == col, 1.0, 0.0)
    return tn(step, eye, HIGH), tn(logd, eye, HIGH)


def down_kernel(uf, ub, top, out):
    out[0] = nn(uf[...], top[0:WIDTH, :])
    out[1] = nn(ub[...], top[0:WIDTH, :])


def front_kernel(which, roster, shared, place, u, part, bottom, up, wt, bias, rate, *refs):
    g, (low_out, v, proj_ref, states) = refs[:N], refs[N:]
    flag = shared[0].astype(F32)
    m = roster[0, which]
    acc = part[which]
    for k in range(N):
        rows = pl.ds(pl.multiple_of(WIDTH + place[k] * SHARD, 16), SHARD)
        acc += tn(g[k][m], bottom[rows, :])
    low = acc.astype(BF16)
    low_out[...] = low
    proj = jnp.zeros((TOK, PROJ), F32)
    for c in range(CHUNKS):
        cols = slice(STEP * c, STEP * (c + 1))
        vc = (u[:, cols].astype(F32) + flag * nn(low, up[:, cols])).astype(BF16)
        v[:, cols] = vc
        proj += nt(vc, wt[:, cols])
    proj_ref[...] = proj
    _, step, keys, _, logd = features(proj, bias[...], rate[...])
    last = logd[TOK - 1 : TOK, :]
    weight = split(jnp.exp(last - logd) * step)
    kb = keys.astype(BF16)
    for c in range(CHUNKS):
        cols = slice(STEP * c, STEP * (c + 1))
        wx = (expand(weight, head_map(c)) * v[:, cols].astype(F32)).astype(BF16)
        store_state(states, c, tn(kb, wx).astype(BF16))
    _, logt = turned(step, logd)
    dec = jnp.broadcast_to(jnp.exp(logt[:, TOK - 1 : TOK]), (HEADS, 128))
    hi, lo = split(dec)
    rr = iota((N * 16, HEADS), 0)
    hh = iota((N * 16, HEADS), 1)
    jj, ii = rr // 16, rr % 16
    bh = (7 * jj + ii) // 4
    bl = (7 * jj + ii - 7) // 4

    def pick(head, ok):
        return jnp.where((hh == head) & ok, 1.0, 0.0).astype(BF16)

    is_hi = ii < 7
    is_lo = (ii >= 7) & (ii < 14)
    even = nn(pick(2 * bh, is_hi), hi) + nn(pick(2 * bl, is_lo), lo)
    odd = nn(pick(2 * bh + 1, is_hi), hi) + nn(pick(2 * bl + 1, is_lo), lo)
    rows = jnp.where(iota((N * 16, 128), 1) < CH, even, odd).astype(BF16)
    for j in range(N):
        states[j, SROWS : SROWS + 16, :] = rows[16 * j : 16 * (j + 1), :]


def store_state(ref, c, st):
    for i in range(STEP // 128):
        for t in range(4):
            tile = 4 * (4 * c + i) + t
            j, r = tile // 7, 16 * (tile % 7)
            ref[j, r : r + 16, :] = st[16 * t : 16 * (t + 1), 128 * i : 128 * (i + 1)]


def state_block(ref, b, base):
    tiles = []
    for t in range(4):
        tile = 4 * b + t
        j, r = tile // 7, base + 16 * (tile % 7)
        tiles.append(ref[j, r : r + 16, :])
    return jnp.concatenate(tiles, axis=0)


def decay_rows(ref, q, base):
    tile = ref[q, base + SROWS : base + SROWS + 16, :].astype(F32)
    return [tile[i : i + 1, :] + tile[7 + i : 8 + i, :] for i in range(7)]


def prefix(s, base, out, out_base):
    run = [jnp.zeros((16, 128), F32) for _ in range(7)]
    for q in range(N):
        dec = decay_rows(s, q, base)
        for i in range(7):
            out[q, out_base + 16 * i : out_base + 16 * (i + 1), :] = run[i].astype(BF16)
            run[i] = run[i] * dec[i] + s[q, base + 16 * i : base + 16 * (i + 1), :].astype(F32)


def prefix_kernel(s, other, out):
    prefix(s, 0, out, 0)
    out[:, SROWS : 2 * SROWS + 16, :] = other[...]


def suffix_kernel(s, ds, out):
    run = [jnp.zeros((16, 128), F32) for _ in range(7)]
    for q in reversed(range(N)):
        dec = decay_rows(s, q, 0)
        for i in range(7):
            rows = slice(16 * i, 16 * (i + 1))
            out[q, rows, :] = run[i].astype(BF16)
            run[i] = run[i] * dec[i] + ds[q, rows, :].astype(F32)


def halves(a):
    first = iota(a.shape, 1) < CH
    zero = jnp.zeros_like(a)
    return jnp.where(first, a, zero), jnp.where(first, zero, a)


def scores_of(queries, keys):
    row = iota((TOK, TOK), 0)
    col = iota((TOK, TOK), 1)
    return jnp.where(row >= col, nt(queries.astype(BF16), keys.astype(BF16)), 0.0)


def fade(logd, logt, stept, h):
    gap = jnp.minimum(logd[:, h : h + 1] - logt[h : h + 1, :], 0.0)
    return jnp.exp(gap) * stept[h : h + 1, :]


def mix_kernel(v, proj, bias, rate, skip, y):
    _, step, keys, queries, logd = features(proj[...], bias[...], rate[...])
    stept, logt = turned(step, logd)
    scores = scores_of(queries, keys)
    for b in range(BLOCKS):
        cols = slice(128 * b, 128 * (b + 1))
        x = v[:, cols]
        x0, x1 = halves(x)
        m0 = (fade(logd, logt, stept, 2 * b) * scores).astype(BF16)
        m1 = (fade(logd, logt, stept, 2 * b + 1) * scores).astype(BF16)
        mix = nn(jnp.concatenate([m0, m1], axis=1), jnp.concatenate([x0, x1], axis=0))
        y[:, cols] = mix + skip[:, cols] * x.astype(F32)


def add_start(part, queries, logd, start, base, y):
    qb = queries.astype(BF16)
    grow = split(jnp.exp(logd))
    total = jnp.zeros((TOK, 128), F32)
    for c in range(CHUNKS):
        grown = expand(grow, head_map(c))
        for i in range(4):
            b = 4 * c + i
            cols = slice(128 * b, 128 * (b + 1))
            inter = nn(qb, state_block(start, b, base)) * grown[:, 128 * i : 128 * (i + 1)]
            res = part[:, cols] + inter
            y[:, cols] = res
            total += res * res
    return lax.rsqrt(jnp.sum(total, axis=1, keepdims=True) / WIDTH + EPS)


def forward_kernel(v, proj, part, start, bias, rate, gain, out, y):
    _, _, _, queries, logd = features(proj[...], bias[...], rate[...])
    r = add_start(part, queries, logd, start, SROWS, y)
    for c in range(CHUNKS):
        cols = slice(STEP * c, STEP * (c + 1))
        out[:, cols] = (v[:, cols].astype(F32) + gain[:, cols] * (y[:, cols] * r)).astype(BF16)


def back_one_kernel(v, proj, part, start, cot, bias, rate, skip, gain, dy_out, ds, rowsum, y):
    prefix(start, SROWS, ds, SROWS)
    _, _, _, queries, logd = features(proj[...], bias[...], rate[...])
    r = add_start(part, queries, logd, start, 0, y)
    along = jnp.zeros((TOK, 128), F32)
    for b in range(BLOCKS):
        cols = slice(128 * b, 128 * (b + 1))
        along += gain[:, cols] * cot[:, cols].astype(F32) * y[:, cols]
    c1 = jnp.sum(along, axis=1, keepdims=True) * (r * r * r / WIDTH)
    qb = queries.astype(BF16)
    grow = split(jnp.exp(logd))
    acc = jnp.zeros((TOK, HEADS), F32)
    for c in range(CHUNKS):
        cols = slice(STEP * c, STEP * (c + 1))
        table = head_map(c)
        yc = y[:, cols]
        dy = (r * (gain[:, cols] * cot[:, cols].astype(F32)) - yc * c1).astype(BF16)
        dy_out[:, cols] = dy
        dyf = dy.astype(F32)
        acc += segment(dyf * (yc - skip[:, cols] * v[:, cols].astype(F32)), table)
        store_state(ds, c, tn(qb, (expand(grow, table) * dyf).astype(BF16)).astype(BF16))
    rowsum[...] = acc


def back_two_kernel(v, proj, start, cot, dy, bias, rate, skip, dvf, col_sum, d_kq):
    _, step, keys, queries, logd = features(proj[...], bias[...], rate[...])
    stept, logt = turned(step, logd)
    scores = scores_of(queries, keys)
    qb = queries.astype(BF16)
    kb = keys.astype(BF16)
    grow = split(jnp.exp(logd))
    d_scores = jnp.zeros((TOK, TOK), F32)
    d_q = jnp.zeros((TOK, CH), F32)
    col_mix = jnp.zeros((TOK, HEADS), F32)
    for c in range(CHUNKS):
        table = head_map(c)
        grown = expand(grow, table)
        parts = []
        for i in range(4):
            b = 4 * c + i
            cols = slice(128 * b, 128 * (b + 1))
            sub = slice(128 * i, 128 * (i + 1))
            x = v[:, cols]
            dyb = dy[:, cols]
            dyf = dyb.astype(F32)
            dy0, dy1 = halves(dyb)
            stacked = jnp.concatenate([dy0, dy1], axis=0)
            f0 = fade(logd, logt, stept, 2 * b)
            f1 = fade(logd, logt, stept, 2 * b + 1)
            m0 = (f0 * scores).astype(BF16)
            m1 = (f1 * scores).astype(BF16)
            d_mix = nt(stacked, x)
            d_scores += d_mix[:TOK] * f0 + d_mix[TOK:] * f1
            dx_mix = tn(jnp.concatenate([m0, m1], axis=0), stacked)
            parts.append(x.astype(F32) * dx_mix)
            d_q += nt((grown[:, sub] * dyf).astype(BF16), state_block(start, b, 0))
            dvf[:, cols] = cot[:, cols].astype(F32) + skip[:, cols] * dyf + dx_mix
        col_mix += segment(jnp.concatenate(parts, axis=1), table)
    row = iota((TOK, TOK), 0)
    col = iota((TOK, TOK), 1)
    d_scores = jnp.where(row >= col, d_scores, 0.0).astype(BF16)
    col_sum[...] = col_mix
    d_kq[0] = tn(d_scores, qb)
    d_kq[1] = d_q + nn(d_scores, kb)


def back_three_kernel(
    roster, shared, place, u, low, v, proj, start, end, dvf0, rowsum, col_sum, d_kq,
    bias, rate, top, up, wt, *refs,
):
    g, (du, keep), give, (dvf, pack, sems) = refs[:N], refs[N : N + 2], refs[N + 2 : N + 6], refs[N + 6 :]
    flag = shared[0].astype(F32)
    core = place[N]
    z, step, keys, _, logd = features(proj[...], bias[...], rate[...])
    kb = keys.astype(BF16)
    last = logd[TOK - 1 : TOK, :]
    weight = split(jnp.exp(last - logd) * step)
    d_k = d_kq[0]
    col_mix = col_sum[...]
    col_state = jnp.zeros((TOK, HEADS), F32)
    d_decay = jnp.zeros((8, HEADS), F32)
    for c in range(CHUNKS):
        table = head_map(c)
        weighed = expand(weight, table)
        parts_state, parts_dec = [], []
        for i in range(4):
            b = 4 * c + i
            cols = slice(128 * b, 128 * (b + 1))
            sub = slice(128 * i, 128 * (i + 1))
            xf = v[:, cols].astype(F32)
            first = state_block(start, b, 0)
            final = state_block(end, b, 0)
            parts_dec.append(
                jnp.sum(first.astype(F32) * final.astype(F32), axis=0, keepdims=True)
            )
            dx_state = nn(kb, final) * weighed[:, sub]
            parts_state.append(xf * dx_state)
            d_k += nt((weighed[:, sub] * xf).astype(BF16), final)
            dvf[:, cols] = dvf0[:, cols] + dx_state
        col_state += segment(jnp.concatenate(parts_state, axis=1), table)
        d_decay += segment(
            jnp.broadcast_to(jnp.concatenate(parts_dec, axis=1), (8, STEP)), table
        )
    row = iota((TOK, TOK), 0)
    col = iota((TOK, TOK), 1)
    d_log = nn(jnp.where(col >= row, 1.0, 0.0), rowsum[...] - col_mix, HIGH)
    d_log += nn(jnp.where(col < row, 1.0, 0.0), col_state, HIGH)
    d_log += jnp.exp(last) * d_decay[0:1, :]
    sig = jax.nn.sigmoid(z)
    ratio = jnp.where(z < -15.0, 1.0, sig / softplus(jnp.maximum(z, -15.0)))
    d_step = (col_mix + col_state) * ratio - rate[...] * d_log * sig
    d_proj = jnp.concatenate([d_step, d_k, d_kq[1]], axis=1).astype(BF16)
    d_main = d_proj[:, 0:128]
    rest = d_proj[:, 128:PROJ]
    blank = jnp.zeros((TOK, 8), BF16)
    half = jnp.concatenate([rest, blank], axis=1)
    none = jnp.zeros((TOK, 64), BF16)
    d_rest = jnp.concatenate([half, none, none, half], axis=1)
    lowv = low[...]
    d_low = jnp.zeros((TOK, RANK), F32)
    slots = (core, 1 - core)

    def store(j, r, rows, value):
        pack[slots[j % 2], j // 2 % 4, j // 8, r : r + rows, :] = value.astype(BF16)

    tiles = {}
    for c in range(CHUNKS):
        cols = slice(STEP * c, STEP * (c + 1))
        dv = (dvf[:, cols] + nn(d_proj, wt[:, cols])).astype(BF16)
        dvf[:, cols] = dv.astype(F32)
        d_low += nt(dv, up[:, cols])
        gb = flag * tn(lowv, dv)
        for j in range(N):
            for i in range(2):
                pair = jnp.concatenate(
                    [gb[8 * j : 8 * j + 8, 128 * (2 * i + k) : 128 * (2 * i + k + 1)] for k in range(2)],
                    axis=0,
                )
                store(j, OFF_B + 16 * (2 * c + i), 16, pair)
        vc = v[:, cols]
        gwa = tn(vc, d_main)
        gwb = tn(vc, d_rest)
        for t in range(STEP // 16):
            tile = (STEP // 16) * c + t
            j, i = tile // 14, tile % 14
            store(j, OFF_WA + 16 * i, 16, gwa[16 * t : 16 * (t + 1)])
            tiles[i] = gwb[16 * t : 16 * (t + 1)]
            if i >= 7:
                both = tiles[i - 7][:, 0:128] + tiles[i][:, 128:256]
                store(j, OFF_WB + 16 * (i - 7), 16, both)
    late = pl.ds(OFF_WA, PACK - OFF_WA)
    early = pl.ds(0, OFF_WA)

    def send(rows, first):
        copies = [pltpu.make_async_copy(pack.at[0, :, :, rows], keep.at[:, :, rows], sems.at[first])]
        for y in range(N // 4):
            copies.append(
                pltpu.make_async_copy(
                    pack.at[1, y, :, rows], give[y].at[:, rows], sems.at[first + 1 + y]
                )
            )
        for copy in copies:
            copy.start()
        return copies

    copies = send(late, 0)
    d_lowb = (flag * d_low).astype(BF16)
    for c in range(CHUNKS):
        cols = slice(STEP * c, STEP * (c + 1))
        du[:, cols] = (dvf[:, cols] + nt(d_lowb, top[cols, :])).astype(BF16)
        ga = tn(u[:, cols], d_lowb)
        for t in range(STEP // 16):
            tile = (STEP // 16) * c + t
            store(tile // 28, 16 * (tile % 28), 16, ga[16 * t : 16 * (t + 1)])
    m = roster[0, 1]
    for k in range(N):
        src = place[k]
        j = src // 2
        slot = (j + core) % 2
        rows = pl.ds(pl.multiple_of((src % 2) * SHARD, 16), SHARD)
        pack[slot, j // 2, 1, rows, :] = nn(g[k][m], d_lowb).astype(BF16)
    copies += send(early, 5)
    for copy in copies:
        copy.wait()


def pair_kernel(keep, *refs):
    taken, out = refs[:-1], refs[-1]
    for q in range(N // 4):
        for h in range(2):
            for r in range(0, PACK, 144):
                rows = slice(r, r + 144)
                both = keep[q, h, rows, :].astype(F32) + taken[q][h, rows, :].astype(F32)
                out[q, h, rows, :] = both.astype(BF16)


def line_kernel(place, p, keep, give):
    for out, h in ((keep, place[N + 1]), (give, 1 - place[N + 1])):
        for r in range(0, PACK, 144):
            rows = slice(r, r + 144)
            acc = p[0, h, rows, :].astype(F32)
            for q in range(1, N // 4):
                acc += p[q, h, rows, :].astype(F32)
            out[rows, :] = acc.astype(BF16)


def copy_kernel(a, out):
    out[...] = a[...]


def last_kernel(keep, taken, ga, gw, gb):
    def total(start, rows):
        part = slice(start, start + rows)
        return keep[part, :].astype(F32) + taken[part, :].astype(F32)

    for i in range(GA // 64):
        ga[64 * i : 64 * (i + 1), :] = total(64 * i, 64).astype(BF16)
    gw[0:128, :] = total(OFF_WA, GWA).T.astype(BF16)
    rest = total(OFF_WB, GWB).T
    gw[128:PROJ, :] = jnp.concatenate([rest[0:56], rest[64:120]], axis=1).astype(BF16)
    for i in range(BLOCKS // 2):
        t = total(OFF_B + 16 * i, 16)
        gb[:, 256 * i : 256 * i + 128] = t[0:8].astype(BF16)
        gb[:, 256 * i + 128 : 256 * (i + 1)] = t[8:16].astype(BF16)


SMEM = pl.BlockSpec(memory_space=pltpu.SMEM)
VMEM = pl.BlockSpec(memory_space=pltpu.VMEM)
ANY = pl.BlockSpec(memory_space=pl.ANY)


def call(kernel, ins, outs, us, scratch=(), smem=0, any_outs=(), after=(), mib=BIG):
    count = len(ins)
    specs = [SMEM if i < smem else VMEM for i in range(count)]
    specs += [ANY] * len(after)

    def body(*refs):
        kernel(*refs[:count], *refs[count + len(after) :])

    return pl.pallas_call(
        body,
        out_shape=[jax.ShapeDtypeStruct(s, d) for s, d in outs],
        in_specs=specs,
        out_specs=[ANY if i in any_outs else VMEM for i in range(len(outs))],
        scratch_shapes=list(scratch),
        compiler_params=pltpu.CompilerParams(vmem_limit_bytes=mib * MIB),
        cost_estimate=pl.CostEstimate(
            flops=int(us * 4e8), bytes_accessed=int(us * 3e6), transcendentals=0
        ),
    )(*ins, *after)


def exchange(a, axis, groups=None):
    return lax.all_to_all(a, axis, 0, 0, axis_index_groups=groups, tiled=True)


def passed_along(value, axis, by):
    devices = lax.axis_size(axis)
    return lax.ppermute(value, axis, [(i, (i + by) % devices) for i in range(devices)])


def swapped(value, by, axis="seq"):
    return lax.ppermute(value, axis, [(i, i ^ by) for i in range(N)])


def ring(own):
    me = lax.axis_index("section")
    pair = me ^ 1
    other = swapped(own, 1, "section")
    blocks, sources = [own, other], [me, pair]
    ahead, behind = [own, other], [own, other]
    for k in range(1, N // 4 + 1):
        for i in range(2):
            ahead[i] = passed_along(ahead[i], "section", 2)
            blocks.append(ahead[i])
            sources.append((me - 2 * k) % N if i == 0 else ((me - 2 * k) % N) ^ 1)
            if k < N // 4:
                behind[i] = passed_along(behind[i], "section", -2)
                blocks.append(behind[i])
                sources.append((me + 2 * k) % N if i == 0 else ((me + 2 * k) % N) ^ 1)
    return blocks, sources


def local(
    forward_layer_inputs,
    backward_layer_inputs,
    output_cotangent,
    embeds,
    roster,
    shared,
    step_key_query_weight,
    head_step_bias,
    rate,
    dskip,
    gain,
    adapter_down_map,
    adapter_up_map,
):
    uf = forward_layer_inputs[0]
    ub = backward_layer_inputs[0]
    cot = output_cotangent[0]
    wt = step_key_query_weight[0].T
    down = adapter_down_map[0]
    up = adapter_up_map[0]
    bias = head_step_bias
    skip = jnp.repeat(dskip, CH, axis=1)
    act = ((TOK, WIDTH), BF16)
    wide = ((TOK, WIDTH), F32)
    scratch = (pltpu.VMEM((TOK, WIDTH), F32),)
    blocks, sources = ring(embeds.transpose(0, 2, 1))
    place = jnp.stack(sources + [lax.axis_index("seq") % 2, lax.axis_index("seq") // 8]).astype(jnp.int32)
    (part,) = call(
        down_kernel, (uf, ub, down), (((2, TOK, RANK), F32),), 3
    )

    def front(which, u):
        def kernel(*refs):
            front_kernel(which, *refs)

        return call(
            kernel,
            (roster, shared, place, u, part, down, up, wt, bias, rate, *blocks),
            (
                ((TOK, RANK), BF16),
                act,
                ((TOK, PROJ), F32),
                ((N, SROWS + 16, 128), BF16),
            ),
            6,
            smem=3,
        )

    def mixed(v, proj):
        return call(mix_kernel, (v, proj, bias, rate, skip), (wide,), 3)[0]

    low_b, v_b, proj_b, states_b = front(1, ub)
    held_b = exchange(states_b, "seq")
    _, v_f, proj_f, states_f = front(0, uf)
    part_b = mixed(v_b, proj_b)
    (begins,) = call(
        prefix_kernel, (held_b, states_f), (((N, 2 * SROWS + 16, 128), BF16),), 1
    )
    start = exchange(begins, "seq")
    part_f = mixed(v_f, proj_f)
    dy, sends, rowsum = call(
        back_one_kernel,
        (v_b, proj_b, part_b, start, cot, bias, rate, skip, gain),
        (act, ((N, 2 * SROWS, 128), BF16), ((TOK, HEADS), F32)),
        4,
        scratch,
        after=(part_f,),
    )
    got = exchange(sends, "seq")
    dvf, col_sum, d_kq = call(
        back_two_kernel,
        (v_b, proj_b, start, cot, dy, bias, rate, skip),
        (wide, ((TOK, HEADS), F32), ((2, TOK, CH), F32)),
        6,
    )
    (ends,) = call(
        suffix_kernel, (held_b, got), (((N, SROWS, 128), BF16),), 1, after=(dvf,)
    )
    end = exchange(ends, "seq")
    (out_f,) = call(
        forward_kernel, (v_f, proj_f, part_f, got, bias, rate, gain), (act,), 3, scratch
    )
    sent_f = passed_along(out_f, "section", 1)
    chips = (N // 4, 2, PACK, 128)
    quarter = ((2, PACK, 128), BF16)
    d_u, keep, *give = call(
        back_three_kernel,
        (
            roster, shared, place, ub, low_b, v_b, proj_b, start, end, dvf, rowsum, col_sum,
            d_kq, bias, rate, down, up, wt, *blocks,
        ),
        (act, (chips, BF16), quarter, quarter, quarter, quarter),
        10,
        scratch + (pltpu.VMEM((2,) + chips, BF16), pltpu.SemaphoreType.DMA((10,))),
        smem=3,
        any_outs=(1, 2, 3, 4, 5),
        after=(out_f,),
    )
    sent_b = passed_along(d_u, "section", -1)
    taken = [swapped(part, 1) for part in give]
    (pairs,) = call(
        pair_kernel, (keep, *taken), ((chips, BF16),), 0.1, mib=SMALL, after=(sent_f,)
    )
    lines = exchange(pairs, "seq", [[8 * h + 2 * y + c for y in range(4)] for h in range(2) for c in range(2)])
    (next_f,) = call(copy_kernel, (sent_f,), (act,), 1)
    half = ((PACK, 128), BF16)
    kept, given = call(line_kernel, (place, lines), (half, half), 1, smem=1, mib=SMALL, after=(next_f,))
    other = swapped(given, 8)
    (prev_b,) = call(copy_kernel, (sent_b,), (act,), 1)
    ga, gw, gb = call(
        last_kernel,
        (kept, other),
        (((GA, RANK), BF16), ((PROJ, GWA), BF16), ((RANK // N, WIDTH), BF16)),
        1,
        mib=SMALL,
        after=(prev_b,),
    )
    return (next_f[None], prev_b[None], gw.T[None], ga[None], gb[None])


def solution(mesh):
    return jax.shard_map(
        local,
        mesh=mesh,
        in_specs=(
            P("section", "seq", None),
            P("section", "seq", None),
            P("section", "seq", None),
            P(None, "seq", "section"),
            P("section", None),
            P("section"),
            P("section", None, None),
            P("section", None),
            P("section", None),
            P("section", None),
            P("section", None),
            P("section", None, None),
            P("section", None, None),
        ),
        out_specs=(
            P("section", "seq", None),
            P("section", "seq", None),
            P("section", "seq", None),
            P("section", "seq", None),
            P("section", "seq", None),
        ),
        check_vma=False,
    )
```
